128 devices in a mesh: grp: 8 (over x, core), loc: 16 (over z, y).
Axes of the slice: x: 4, y: 4, z: 4, core: 2. Of those that a mesh axis runs over, the one named last changes fastest.
Arguments:
- tokens: bfloat16 [16384, 2048], P(('grp', 'loc')), may hold values from -6 to 6
- expert_ids: int32 [16384, 2], P(('grp', 'loc')), may hold values from 0 to 127, all different within a row; in each aligned block of 128 rows (0 to 127, 128 to 255, ...) at most 4 rows name the same one
- gate_fixed: int32 [16384, 2], P(('grp', 'loc')), may hold values from 1 to 4096
- gate_weight: bfloat16 [128, 2048, 1024], P(('grp', 'loc')), may hold values from -0.125 to 0.125
- up_weight: bfloat16 [128, 2048, 1024], P(('grp', 'loc')), may hold values from -0.125 to 0.125
- down_weight: bfloat16 [128, 1024, 2048], P(('grp', 'loc')), may hold values from -0.1875 to 0.1875
Outputs:
- mixed: bfloat16 [16384, 2048], P(('grp', 'loc'))
The draws below stay inside these ranges and needn't reach their ends.
Inputs may be any that keep to these rules, and one draw needn't show every extreme that they name: `expert_ids`: each row names two different experts; among the rows of one device no expert is named more than 4 times, and one is named exactly 4 times.
All inputs are finite; a program needn't handle non-finite values.
Results may differ from the reference program's by a relative error of at most 0.0058.
Values may be sent and summed in bfloat16 or wider, within the bound.
A program may use at most 64 MiB of HBM per device.

```python
import math
import jax
import jax.numpy as jnp
import numpy as np
from jax import lax

D = 2048
FF = 1024
TOK_DEV = 128
TOKENS = 16384
EXPERTS = 128
CAP = 4
N_GRP = 8
N_LOC = 16


def with_ends(values, rng, least, largest):
    shape = values.shape
    place = [jax.random.randint(jax.random.fold_in(rng, axis), (), 0, shape[axis]) for axis in range(len(shape))]
    values = values.at[tuple(place)].set(least)
    longest = shape.index(max(shape))
    place[longest] = (place[longest] + 1) % shape[longest]
    return values.at[tuple(place)].set(largest)


def shard_levels(key, shape, split, smallest, largest):
    level = 1.0
    for axis_at, shards_of in split:
        draws = jax.random.uniform(jax.random.fold_in(jax.random.fold_in(key, 6), axis_at), (shards_of,), jnp.float32, smallest / len(split), largest / len(split))
        level = level * jnp.repeat(jnp.exp(draws), shape[axis_at] // shards_of).reshape((-1,) + (1,) * (len(shape) - 1 - axis_at))
    return level


def shared_out(rng, own, number, rows, count, top, most, skew):
    ranking = jax.random.permutation(rng, count)
    heavy_load, usual = portions_of(count, rows * top, most, skew, True), portions_of(count, rows * top, most, skew, False)
    places = jnp.arange(count)

    def named(lengths, turn):
        used = int((lengths > 0).sum())
        fixed = max(1, used // 4)
        passed = fixed + (places - fixed + turn * (used - fixed)) % max(1, count - fixed)
        return jnp.zeros((count,), jnp.int32).at[ranking[jnp.where(places < fixed, places, passed)]].set(jnp.asarray(lengths, jnp.int32))

    lengths = jnp.where(number % 4 == 0, named(heavy_load, number // 4), named(usual, number - number // 4 - 1))
    mixed = jax.random.permutation(jax.random.fold_in(own, 3), count)
    donor, sink = mixed[0:count // 2 * 2:2], mixed[1:count // 2 * 2:2]
    room = jnp.minimum(lengths[donor] - 1, most - lengths[sink]) // 2
    room = jnp.where((donor == ranking[0]) | (sink == ranking[0]) | (lengths[sink] == 0), 0, jnp.maximum(room, 0))
    passed = jax.random.randint(jax.random.fold_in(own, 4), (count // 2,), 0, 1 << 20) % (room + 1)
    lengths = lengths.at[donor].add(-passed).at[sink].add(passed)
    members = jnp.searchsorted(jnp.cumsum(lengths), jnp.arange(rows * top), side="right").astype(jnp.int32)
    listing = members.reshape(top, rows).T
    listing = listing[jax.random.permutation(jax.random.fold_in(own, 1), rows)]
    turn = jax.random.randint(jax.random.fold_in(own, 2), (rows, 1), 0, top)
    return jnp.take_along_axis(listing, (jnp.arange(top)[None, :] + turn) % top, axis=1)


def portions_of(number_of, total, limit, skew, full):
    weights = [(1 << 20) // math.isqrt(standing ** skew) + 1 for standing in range(1, number_of + 1)]
    largest = limit if full else min(limit, max(-(-total // number_of), total * weights[0] // sum(weights)))
    least = 1 if total - largest >= number_of - 1 else 0
    given, rest = [largest] + [least] * (number_of - 1), total - largest - least * (number_of - 1)
    while rest > 0:
        movable = [i for i in range(1, number_of) if given[i] < largest] or [i for i in range(1, number_of) if given[i] < limit]
        whole, budget = sum([weights[i] for i in movable]), rest
        for i in movable:
            more = min(limit - given[i], max(1, budget * weights[i] // whole), rest)
            given[i] = given[i] + more
            rest = rest - more
    return np.array(given)


def scatter_about(own_key, shape, deviation, most, shards=(), kind=jnp.bfloat16):
    gain = shard_levels(own_key, shape, shards, -0.22, 0.18) if shards else 1.0
    entries = jax.random.normal(own_key, shape, jnp.float32) * deviation * gain
    return jnp.minimum(jnp.maximum(entries, -most), most).astype(kind)


def setup_inputs(seed: int = 0) -> dict:
    streams_of = jax.random.split(jax.random.key(seed), 7)
    tokens = scatter_about(streams_of[0], (TOKENS, D), 1.0, 6.0, ((0, 128),))
    expert_ids_keys = jax.random.split(jax.random.fold_in(streams_of[1], 1), TOKENS // TOK_DEV)
    expert_ids_turns = jax.random.permutation(jax.random.fold_in(streams_of[1], 3), TOKENS // TOK_DEV)
    expert_ids = jax.vmap(lambda own, number: shared_out(jax.random.fold_in(streams_of[1], 2), own, number, TOK_DEV, EXPERTS, 2, CAP, 2))(expert_ids_keys, expert_ids_turns).reshape((TOKENS, 2))
    gate_fixed = with_ends(jax.random.randint(streams_of[2], (TOKENS, 2), 1, 4097), jax.random.fold_in(streams_of[2], 1), 1, 4096).astype(jnp.int32)
    gate_weight = scatter_about(streams_of[3], (EXPERTS, D, FF), D ** -0.5, 0.125, ((0, 128),))
    up_weight = scatter_about(streams_of[4], (EXPERTS, D, FF), D ** -0.5, 0.125, ((0, 128),))
    down_weight = scatter_about(streams_of[5], (EXPERTS, FF, D), FF ** -0.5, 0.1875, ((0, 128),))
    return {"tokens": tokens, "expert_ids": expert_ids, "gate_fixed": gate_fixed, "gate_weight": gate_weight, "up_weight": up_weight, "down_weight": down_weight}


def expert_rows(rows, w_gate, w_up, w_down):
    gate = jnp.dot(rows, w_gate, preferred_element_type=jnp.float32)
    upper = jnp.dot(rows, w_up, preferred_element_type=jnp.float32)
    hidden = (jax.nn.silu(gate) * upper).astype(jnp.bfloat16)
    return jnp.dot(hidden, w_down, preferred_element_type=jnp.float32).astype(jnp.bfloat16)


def reference(tokens, expert_ids, gate_fixed, gate_weight, up_weight, down_weight):
    fixed = gate_fixed.astype(jnp.float32)
    weights = (fixed / jnp.sum(fixed, axis=1, keepdims=True)).reshape(-1)
    flat_ids = expert_ids.reshape(-1).astype(jnp.int32)
    order = jnp.argsort(flat_ids, stable=True).astype(jnp.int32)
    ordered = flat_ids[order]
    expert_range = jnp.arange(EXPERTS, dtype=jnp.int32)
    starts = jnp.searchsorted(ordered, expert_range, side="left").astype(jnp.int32)
    ends = jnp.searchsorted(ordered, expert_range, side="right").astype(jnp.int32)
    reach = N_GRP * N_LOC * CAP
    padded = jnp.concatenate([order, jnp.zeros((reach,), jnp.int32)])
    positions = jnp.arange(reach, dtype=jnp.int32)

    def visit(expert, total):
        picked = lax.dynamic_slice_in_dim(padded, starts[expert], reach)
        valid = (positions < ends[expert] - starts[expert]).astype(jnp.float32)
        token_rows = picked // 2
        result = expert_rows(tokens[token_rows], gate_weight[expert], up_weight[expert], down_weight[expert])
        scale = weights[picked] * valid
        return total.at[token_rows].add(result.astype(jnp.float32) * scale[:, None])

    total = lax.fori_loop(0, EXPERTS, visit, jnp.zeros((TOKENS, D), jnp.float32))
    return total.astype(jnp.bfloat16)
```

```python
import functools

import jax
import jax.numpy as jnp
import numpy as np
from jax import lax
from jax.experimental import pallas as pl
from jax.experimental.pallas import tpu as pltpu
from jax.sharding import PartitionSpec as P

MESH = pl.DeviceIdType.MESH
CAP = 4
CHUNKS = 4


def far(offset):
    return sum(min(step, 4 - step) for step in (offset[0], offset[2], offset[3]))


OFFSETS = sorted(
    ((dx, dc, dz, dy) for dx in range(4) for dc in range(2) for dz in range(4) for dy in range(4) if dx + dc + dz + dy),
    key=lambda offset: -far(offset),
) + [(0, 0, 0, 0)]
N = len(OFFSETS)
PER = N // CHUNKS
ROWS = PER * CAP


def place():
    grp, loc = lax.axis_index("grp"), lax.axis_index("loc")
    return grp // 2, grp % 2, loc // 4, loc % 4


def device_at(offset, sign):
    x, c, z, y = place()
    dx, dc, dz, dy = offset
    return (
        (x + sign * dx + 4) % 4 * 2 + (c + dc) % 2,
        (z + sign * dz + 4) % 4 * 4 + (y + sign * dy + 4) % 4,
    )


def kernel(
    tokens, ids, gates, table, w_gate, w_up, w_down, out,
    gate_v, up_v, down_v, send, recv, ret, back, mix, total,
    weight_sem, send_sem, recv_sem, ret_sem, back_sem, own_sem,
):
    barrier = pltpu.get_barrier_semaphore()
    for offset in OFFSETS[:-1]:
        pl.semaphore_signal(barrier, 1, device_id=device_at(offset, 1), device_id_type=MESH)
    loads = [
        pltpu.make_async_copy(src.at[0], dst, weight_sem.at[i])
        for i, (src, dst) in enumerate(((w_gate, gate_v), (w_up, up_v), (w_down, down_v)))
    ]
    for load in loads:
        load.start()

    x, c, z, y = place()
    expert = ((x + table[0:1, :]) % 4 * 2 + (c + table[1:2, :]) % 2) * 16
    expert = expert + (z + table[2:3, :]) % 4 * 4 + (y + table[3:4, :]) % 4
    first = ids[:, 0:1] == expert
    second = ids[:, 1:2] == expert
    named = first | second
    rows = tokens.shape[0]
    lower = lax.broadcasted_iota(jnp.int32, (rows, rows), 0) > lax.broadcasted_iota(jnp.int32, (rows, rows), 1)
    before = jnp.dot(
        lower.astype(jnp.bfloat16), named.astype(jnp.bfloat16), preferred_element_type=jnp.float32
    )
    chosen = named & (before == table[4:5, :].astype(jnp.float32))
    fixed = gates[...].astype(jnp.float32)
    weights = fixed / jnp.sum(fixed, axis=1, keepdims=True)
    scale = jnp.where(chosen, jnp.where(first, weights[:, 0:1], weights[:, 1:2]), 0.0)
    mix[0] = scale.astype(jnp.bfloat16)
    mix[1] = (scale - mix[0].astype(jnp.float32)).astype(jnp.bfloat16)
    pick = jnp.where(chosen, 1.0, 0.0).astype(jnp.bfloat16)
    for k in range(CHUNKS):
        part = lax.dot_general(
            pick[:, k * ROWS : (k + 1) * ROWS], tokens[...], (((0,), (0,)), ((), ())), preferred_element_type=jnp.float32
        )
        send[k * PER : (k + 1) * PER] = part.astype(jnp.bfloat16).reshape(PER, CAP, -1)

    pl.semaphore_wait(barrier, N - 1)
    own = pltpu.make_async_copy(send.at[N - 1], recv.at[N - 1], own_sem.at[0])
    for i, offset in enumerate(OFFSETS[:-1]):
        pltpu.make_async_remote_copy(
            send.at[i], recv.at[i], send_sem, recv_sem.at[i // PER],
            device_id=device_at(offset, 1), device_id_type=MESH,
        ).start()
    own.start()
    for load in loads:
        load.wait()

    def arrived(buffer, sem, k):
        count = PER - (k == CHUNKS - 1)
        landed = buffer.at[pl.ds(k * PER, count)]
        pltpu.make_async_copy(landed, landed, sem.at[k]).wait()

    for k in range(CHUNKS):
        arrived(recv, recv_sem, k)
        if k == CHUNKS - 1:
            own.wait()
        block = recv[k * PER : (k + 1) * PER].reshape(ROWS, -1)
        gate = jnp.dot(block, gate_v[...], preferred_element_type=jnp.float32)
        upper = jnp.dot(block, up_v[...], preferred_element_type=jnp.float32)
        hidden = (gate / (1.0 + jnp.exp(-gate)) * upper).astype(jnp.bfloat16)
        result = jnp.dot(hidden, down_v[...], preferred_element_type=jnp.float32)
        ret[k * PER : (k + 1) * PER] = result.astype(jnp.bfloat16).reshape(PER, CAP, -1)
        for i in range(k * PER, min((k + 1) * PER, N - 1)):
            pltpu.make_async_remote_copy(
                ret.at[i], back.at[i], ret_sem, back_sem.at[k],
                device_id=device_at(OFFSETS[i], -1), device_id_type=MESH,
            ).start()
    home = pltpu.make_async_copy(ret.at[N - 1], back.at[N - 1], own_sem.at[1])
    home.start()

    for k in range(CHUNKS):
        arrived(back, back_sem, k)
        if k == CHUNKS - 1:
            home.wait()
        block = back[k * PER : (k + 1) * PER].reshape(ROWS, -1)
        columns = slice(k * ROWS, (k + 1) * ROWS)
        part = jnp.dot(mix[0, :, columns], block, preferred_element_type=jnp.float32)
        part = part + jnp.dot(mix[1, :, columns], block, preferred_element_type=jnp.float32)
        total[...] = part if k == 0 else total[...] + part
    out[...] = total[...].astype(out.dtype)
    sent = send.at[pl.ds(0, N - 1)]
    pltpu.make_async_copy(sent, sent, send_sem).wait()
    pltpu.make_async_copy(sent, sent, ret_sem).wait()


def body(tokens, expert_ids, gate_fixed, gate_weight, up_weight, down_weight):
    rows, width = tokens.shape
    hidden = gate_weight.shape[2]
    table = np.zeros((8, N * CAP), np.int32)
    for i, offset in enumerate(OFFSETS):
        for j in range(CAP):
            table[:4, i * CAP + j] = offset
            table[4, i * CAP + j] = j
    vmem = pl.BlockSpec(memory_space=pltpu.VMEM)
    hbm = pl.BlockSpec(memory_space=pl.ANY)
    slots = pltpu.VMEM((N, CAP, width), jnp.bfloat16)
    dma = pltpu.SemaphoreType.DMA
    return pl.pallas_call(
        kernel,
        out_shape=jax.ShapeDtypeStruct((rows, width), jnp.bfloat16),
        in_specs=[vmem] * 4 + [hbm] * 3,
        out_specs=vmem,
        scratch_shapes=[
            pltpu.VMEM((width, hidden), jnp.bfloat16),
            pltpu.VMEM((width, hidden), jnp.bfloat16),
            pltpu.VMEM((hidden, width), jnp.bfloat16),
            slots, slots, slots, slots,
            pltpu.VMEM((2, rows, N * CAP), jnp.bfloat16),
            pltpu.VMEM((rows, width), jnp.float32),
            dma((3,)), dma, dma((CHUNKS,)), dma, dma((CHUNKS,)), dma((2,)),
        ],
        compiler_params=pltpu.CompilerParams(
            collective_id=0, has_side_effects=True, vmem_limit_bytes=56 << 20
        ),
    )(tokens, expert_ids, gate_fixed, jnp.asarray(table), gate_weight, up_weight, down_weight)


def solution(mesh):
    rows = P(("grp", "loc"), None)
    experts = P(("grp", "loc"), None, None)
    return jax.shard_map(
        body, mesh=mesh, in_specs=(rows, rows, rows, experts, experts, experts), out_specs=rows, check_vma=False
    )
```

```python
import functools

import jax
import jax.numpy as jnp
import numpy as np
from jax import lax
from jax.experimental import pallas as pl
from jax.experimental.pallas import tpu as pltpu
from jax.sharding import PartitionSpec as P

MESH = pl.DeviceIdType.MESH
CAP = 4
CHUNKS = 4


def far(offset):
    return sum(min(step, 4 - step) for step in (offset[0], offset[2], offset[3]))


OFFSETS = sorted(
    ((dx, dc, dz, dy) for dx in range(4) for dc in range(2) for dz in range(4) for dy in range(4) if dx + dc + dz + dy),
    key=lambda offset: -far(offset),
) + [(0, 0, 0, 0)]
N = len(OFFSETS)
PER = N // CHUNKS
ROWS = PER * CAP


def place():
    grp, loc = lax.axis_index("grp"), lax.axis_index("loc")
    return grp // 2, grp % 2, loc // 4, loc % 4


def device_at(offset, sign):
    x, c, z, y = place()
    dx, dc, dz, dy = offset
    return (
        (x + sign * dx + 4) % 4 * 2 + (c + dc) % 2,
        (z + sign * dz + 4) % 4 * 4 + (y + sign * dy + 4) % 4,
    )


def spread(index):
    return index % 4 + index // 4 % 4 * 8 + index // 16 % 2 * 64 + index // 32 * 256


def kernel(
    tokens, ids, gates, table, w_gate, w_up, w_down, out,
    tokens_v, ids_v, gates_v, table_v, gate_v, up_v, down_v, send, recv, ret, back, mix, total,
    load_sem, send_sem, recv_sem, ret_sem, back_sem, own_sem,
):
    barrier = pltpu.get_barrier_semaphore()
    for offset in OFFSETS[:-1]:
        pl.semaphore_signal(barrier, 1, device_id=device_at(offset, 1), device_id_type=MESH)
    loads = [
        pltpu.make_async_copy(src, dst, load_sem.at[i])
        for i, (src, dst) in enumerate((
            (ids, ids_v), (table, table_v), (gates, gates_v), (tokens, tokens_v),
            (w_gate.at[0], gate_v), (w_up.at[0], up_v), (w_down.at[0], down_v),
        ))
    ]
    for load in loads:
        load.start()

    x, c, z, y = place()
    for load in loads[:3]:
        load.wait()
    expert = (table_v[...] + spread(x * 32 + c * 16 + z * 4 + y)) & spread(N - 1)
    asked = spread(ids_v[...])
    first = asked[0:1, :] == expert
    second = asked[1:2, :] == expert
    named = first | second
    rows = tokens.shape[0]
    earlier = lax.broadcasted_iota(jnp.int32, (rows, rows), 0) < lax.broadcasted_iota(jnp.int32, (rows, rows), 1)
    before = jnp.dot(
        named.astype(jnp.bfloat16), earlier.astype(jnp.bfloat16), preferred_element_type=jnp.float32
    )
    slot = lax.broadcasted_iota(jnp.int32, named.shape, 0) % CAP
    chosen = named & (before == slot.astype(jnp.float32))
    pick = chosen.astype(jnp.bfloat16)
    loads[3].wait()
    for k in range(CHUNKS):
        part = jnp.dot(pick[k * ROWS : (k + 1) * ROWS], tokens_v[...], preferred_element_type=jnp.float32)
        send[k * PER : (k + 1) * PER] = part.astype(jnp.bfloat16).reshape(PER, CAP, -1)
        if k == 0:
            pl.semaphore_wait(barrier, N - 1)
        for i in range(k * PER, min((k + 1) * PER, N - 1)):
            pltpu.make_async_remote_copy(
                send.at[i], recv.at[i], send_sem, recv_sem.at[k],
                device_id=device_at(OFFSETS[i], 1), device_id_type=MESH,
            ).start()
    own = pltpu.make_async_copy(send.at[N - 1], recv.at[N - 1], own_sem.at[0])
    own.start()

    fixed = gates_v[...].astype(jnp.float32)
    weights = fixed / jnp.sum(fixed, axis=0, keepdims=True)
    scale = jnp.where(chosen, jnp.where(first, weights[0:1, :], weights[1:2, :]), 0.0).T
    mix[0] = scale.astype(jnp.bfloat16)
    mix[1] = (scale - mix[0].astype(jnp.float32)).astype(jnp.bfloat16)
    for load in loads[4:]:
        load.wait()

    def arrived(buffer, sem, k):
        count = PER - (k == CHUNKS - 1)
        landed = buffer.at[pl.ds(k * PER, count)]
        pltpu.make_async_copy(landed, landed, sem.at[k]).wait()

    for k in range(CHUNKS):
        arrived(recv, recv_sem, k)
        if k == CHUNKS - 1:
            own.wait()
        block = recv[k * PER : (k + 1) * PER].reshape(ROWS, -1)
        gate = jnp.dot(block, gate_v[...], preferred_element_type=jnp.float32)
        upper = jnp.dot(block, up_v[...], preferred_element_type=jnp.float32)
        hidden = (gate / (1.0 + jnp.exp(-gate)) * upper).astype(jnp.bfloat16)
        result = jnp.dot(hidden, down_v[...], preferred_element_type=jnp.float32)
        ret[k * PER : (k + 1) * PER] = result.astype(jnp.bfloat16).reshape(PER, CAP, -1)
        for i in range(k * PER, min((k + 1) * PER, N - 1)):
            pltpu.make_async_remote_copy(
                ret.at[i], back.at[i], ret_sem, back_sem.at[k],
                device_id=device_at(OFFSETS[i], -1), device_id_type=MESH,
            ).start()
    home = pltpu.make_async_copy(ret.at[N - 1], back.at[N - 1], own_sem.at[1])
    home.start()

    for k in range(CHUNKS):
        arrived(back, back_sem, k)
        if k == CHUNKS - 1:
            home.wait()
        block = back[k * PER : (k + 1) * PER].reshape(ROWS, -1)
        columns = slice(k * ROWS, (k + 1) * ROWS)
        part = jnp.dot(mix[0, :, columns], block, preferred_element_type=jnp.float32)
        part = part + jnp.dot(mix[1, :, columns], block, preferred_element_type=jnp.float32)
        if k == CHUNKS - 1:
            out[...] = (total[...] + part).astype(out.dtype)
        else:
            total[...] = part if k == 0 else total[...] + part
    sent = send.at[pl.ds(0, N - 1)]
    pltpu.make_async_copy(sent, sent, send_sem).wait()
    pltpu.make_async_copy(sent, sent, ret_sem).wait()


def body(tokens, expert_ids, gate_fixed, gate_weight, up_weight, down_weight):
    rows, width = tokens.shape
    hidden = gate_weight.shape[2]
    table = np.zeros((N * CAP, rows), np.int32)
    for i, (dx, dc, dz, dy) in enumerate(OFFSETS):
        table[i * CAP : (i + 1) * CAP] = spread(dx * 32 + dc * 16 + dz * 4 + dy)
    vmem = pl.BlockSpec(memory_space=pltpu.VMEM)
    hbm = pl.BlockSpec(memory_space=pl.ANY)
    slots = pltpu.VMEM((N, CAP, width), jnp.bfloat16)
    dma = pltpu.SemaphoreType.DMA
    return pl.pallas_call(
        kernel,
        out_shape=pltpu.VMEM((rows, width), jnp.bfloat16),
        in_specs=[hbm] * 7,
        out_specs=vmem,
        scratch_shapes=[
            pltpu.VMEM((rows, width), jnp.bfloat16),
            pltpu.VMEM((2, rows), jnp.int32),
            pltpu.VMEM((2, rows), jnp.int32),
            pltpu.VMEM((N * CAP, rows), jnp.int32),
            pltpu.VMEM((width, hidden), jnp.bfloat16),
            pltpu.VMEM((width, hidden), jnp.bfloat16),
            pltpu.VMEM((hidden, width), jnp.bfloat16),
            slots, slots, slots, slots,
            pltpu.VMEM((2, rows, N * CAP), jnp.bfloat16),
            pltpu.VMEM((rows, width), jnp.float32),
            dma((7,)), dma, dma((CHUNKS,)), dma, dma((CHUNKS,)), dma((2,)),
        ],
        compiler_params=pltpu.CompilerParams(
            collective_id=0, has_side_effects=True, vmem_limit_bytes=60 << 20
        ),
    )(tokens, expert_ids.T, gate_fixed.T, jnp.asarray(table), gate_weight, up_weight, down_weight)


def solution(mesh):
    rows = P(("grp", "loc"), None)
    experts = P(("grp", "loc"), None, None)
    return jax.shard_map(
        body, mesh=mesh, in_specs=(rows, rows, rows, experts, experts, experts), out_specs=rows, check_vma=False
    )
```

```python
import functools

import jax
import jax.numpy as jnp
import numpy as np
from jax import lax
from jax.experimental import pallas as pl
from jax.experimental.pallas import tpu as pltpu
from jax.sharding import PartitionSpec as P

MESH = pl.DeviceIdType.MESH
CAP = 4
CHUNKS = 4


def far(offset):
    return sum(min(step, 4 - step) for step in (offset[0], offset[2], offset[3]))


def turns(offset):
    return (offset[0] + offset[1] > 0) + (offset[2] > 0) + (offset[3] > 0)


OFFSETS = sorted(
    ((dx, dc, dz, dy) for dx in range(4) for dc in range(2) for dz in range(4) for dy in range(4) if dx + dc + dz + dy),
    key=lambda offset: (turns(offset) == 3, -far(offset)),
) + [(0, 0, 0, 0)]
N = len(OFFSETS)
NEAR = [offset for offset in OFFSETS[:-1] if turns(offset) < 3]
COLUMN = [(0, 0, dz, 0) for dz in range(1, 4)]
PER = N // CHUNKS
ROWS = PER * CAP


def place():
    grp, loc = lax.axis_index("grp"), lax.axis_index("loc")
    return grp // 2, grp % 2, loc // 4, loc % 4


def device_at(offset, sign):
    x, c, z, y = place()
    dx, dc, dz, dy = offset
    return (
        (x + sign * dx + 4) % 4 * 2 + (c + dc) % 2,
        (z + sign * dz + 4) % 4 * 4 + (y + sign * dy + 4) % 4,
    )


def spread(index):
    return index % 4 + index // 4 % 4 * 8 + index // 16 % 2 * 64 + index // 32 * 256


def kernel(
    tokens, ids, gates, table, w_gate, w_up, w_down, out,
    tokens_v, ids_v, gates_v, table_v, gate_v, up_v, down_v, send, recv, ret, back, mix, total,
    load_sem, send_sem, recv_sem, ret_sem, back_sem, own_sem, rest_sem,
):
    barrier = pltpu.get_barrier_semaphore()
    for offset in NEAR:
        pl.semaphore_signal(barrier, 1, device_id=device_at(offset, 1), device_id_type=MESH)
    loads = [
        pltpu.make_async_copy(src, dst, load_sem.at[i])
        for i, (src, dst) in enumerate((
            (ids, ids_v), (table, table_v), (gates, gates_v), (tokens, tokens_v),
            (w_gate.at[0], gate_v), (w_up.at[0], up_v), (w_down.at[0], down_v),
        ))
    ]
    for load in loads:
        load.start()

    x, c, z, y = place()
    for load in loads[:3]:
        load.wait()
    expert = (table_v[...] + spread(x * 32 + c * 16 + z * 4 + y)) & spread(N - 1)
    asked = spread(ids_v[...])
    first = asked[0:1, :] == expert
    second = asked[1:2, :] == expert
    named = first | second
    rows = tokens.shape[0]
    earlier = lax.broadcasted_iota(jnp.int32, (rows, rows), 0) < lax.broadcasted_iota(jnp.int32, (rows, rows), 1)
    before = jnp.dot(
        named.astype(jnp.bfloat16), earlier.astype(jnp.bfloat16), preferred_element_type=jnp.float32
    )
    slot = lax.broadcasted_iota(jnp.int32, named.shape, 0) % CAP
    chosen = named & (before == slot.astype(jnp.float32))
    pick = chosen.astype(jnp.bfloat16)
    loads[3].wait()
    for k in range(CHUNKS):
        part = jnp.dot(pick[k * ROWS : (k + 1) * ROWS], tokens_v[...], preferred_element_type=jnp.float32)
        send[k * PER : (k + 1) * PER] = part.astype(jnp.bfloat16).reshape(PER, CAP, -1)
        if k == 0:
            pl.semaphore_wait(barrier, len(NEAR))
            for offset in COLUMN:
                pl.semaphore_signal(rest_sem, 1, device_id=device_at(offset, 1), device_id_type=MESH)
        if (k + 1) * PER > len(NEAR) >= k * PER:
            pl.semaphore_wait(rest_sem, len(COLUMN))
        for i in range(k * PER, min((k + 1) * PER, N - 1)):
            pltpu.make_async_remote_copy(
                send.at[i], recv.at[i], send_sem, recv_sem.at[k],
                device_id=device_at(OFFSETS[i], 1), device_id_type=MESH,
            ).start()
    own = pltpu.make_async_copy(send.at[N - 1], recv.at[N - 1], own_sem.at[0])
    own.start()

    fixed = gates_v[...].astype(jnp.float32)
    weights = fixed / jnp.sum(fixed, axis=0, keepdims=True)
    scale = jnp.where(chosen, jnp.where(first, weights[0:1, :], weights[1:2, :]), 0.0).T
    mix[0] = scale.astype(jnp.bfloat16)
    mix[1] = (scale - mix[0].astype(jnp.float32)).astype(jnp.bfloat16)
    for load in loads[4:]:
        load.wait()

    def arrived(buffer, sem, k):
        count = PER - (k == CHUNKS - 1)
        landed = buffer.at[pl.ds(k * PER, count)]
        pltpu.make_async_copy(landed, landed, sem.at[k]).wait()

    for k in range(CHUNKS):
        arrived(recv, recv_sem, k)
        if k == CHUNKS - 1:
            own.wait()
        block = recv[k * PER : (k + 1) * PER].reshape(ROWS, -1)
        gate = jnp.dot(block, gate_v[...], preferred_element_type=jnp.float32)
        upper = jnp.dot(block, up_v[...], preferred_element_type=jnp.float32)
        hidden = (gate / (1.0 + jnp.exp(-gate)) * upper).astype(jnp.bfloat16)
        result = jnp.dot(hidden, down_v[...], preferred_element_type=jnp.float32)
        ret[k * PER : (k + 1) * PER] = result.astype(jnp.bfloat16).reshape(PER, CAP, -1)
        for i in range(k * PER, min((k + 1) * PER, N - 1)):
            pltpu.make_async_remote_copy(
                ret.at[i], back.at[i], ret_sem, back_sem.at[k],
                device_id=device_at(OFFSETS[i], -1), device_id_type=MESH,
            ).start()
    home = pltpu.make_async_copy(ret.at[N - 1], back.at[N - 1], own_sem.at[1])
    home.start()

    for k in range(CHUNKS):
        arrived(back, back_sem, k)
        if k == CHUNKS - 1:
            home.wait()
        block = back[k * PER : (k + 1) * PER].reshape(ROWS, -1)
        columns = slice(k * ROWS, (k + 1) * ROWS)
        part = jnp.dot(mix[0, :, columns], block, preferred_element_type=jnp.float32)
        part = part + jnp.dot(mix[1, :, columns], block, preferred_element_type=jnp.float32)
        if k == CHUNKS - 1:
            out[...] = (total[...] + part).astype(out.dtype)
        else:
            total[...] = part if k == 0 else total[...] + part
    sent = send.at[pl.ds(0, N - 1)]
    pltpu.make_async_copy(sent, sent, send_sem).wait()
    pltpu.make_async_copy(sent, sent, ret_sem).wait()


def body(tokens, expert_ids, gate_fixed, gate_weight, up_weight, down_weight):
    rows, width = tokens.shape
    hidden = gate_weight.shape[2]
    table = np.zeros((N * CAP, rows), np.int32)
    for i, (dx, dc, dz, dy) in enumerate(OFFSETS):
        table[i * CAP : (i + 1) * CAP] = spread(dx * 32 + dc * 16 + dz * 4 + dy)
    vmem = pl.BlockSpec(memory_space=pltpu.VMEM)
    hbm = pl.BlockSpec(memory_space=pl.ANY)
    slots = pltpu.VMEM((N, CAP, width), jnp.bfloat16)
    dma = pltpu.SemaphoreType.DMA
    return pl.pallas_call(
        kernel,
        out_shape=pltpu.VMEM((rows, width), jnp.bfloat16),
        in_specs=[hbm] * 7,
        out_specs=vmem,
        scratch_shapes=[
            pltpu.VMEM((rows, width), jnp.bfloat16),
            pltpu.VMEM((2, rows), jnp.int32),
            pltpu.VMEM((2, rows), jnp.int32),
            pltpu.VMEM((N * CAP, rows), jnp.int32),
            pltpu.VMEM((width, hidden), jnp.bfloat16),
            pltpu.VMEM((width, hidden), jnp.bfloat16),
            pltpu.VMEM((hidden, width), jnp.bfloat16),
            slots, slots, slots, slots,
            pltpu.VMEM((2, rows, N * CAP), jnp.bfloat16),
            pltpu.VMEM((rows, width), jnp.float32),
            dma((7,)), dma, dma((CHUNKS,)), dma, dma((CHUNKS,)), dma((2,)), pltpu.SemaphoreType.REGULAR,
        ],
        compiler_params=pltpu.CompilerParams(
            collective_id=0, has_side_effects=True, vmem_limit_bytes=60 << 20
        ),
    )(tokens, expert_ids.T, gate_fixed.T, jnp.asarray(table), gate_weight, up_weight, down_weight)


def solution(mesh):
    rows = P(("grp", "loc"), None)
    experts = P(("grp", "loc"), None, None)
    return jax.shard_map(
        body, mesh=mesh, in_specs=(rows, rows, rows, experts, experts, experts), out_specs=rows, check_vma=False
    )
```

```python
import functools

import jax
import jax.numpy as jnp
import numpy as np
from jax import lax
from jax.experimental import pallas as pl
from jax.experimental.pallas import tpu as pltpu
from jax.sharding import PartitionSpec as P

MESH = pl.DeviceIdType.MESH
CAP = 4
CHUNKS = 4


def far(offset):
    return sum(min(step, 4 - step) for step in (offset[0], offset[2], offset[3]))


def turns(offset):
    return (offset[0] + offset[1] > 0) + (offset[2] > 0) + (offset[3] > 0)


OFFSETS = sorted(
    ((dx, dc, dz, dy) for dx in range(4) for dc in range(2) for dz in range(4) for dy in range(4) if dx + dc + dz + dy),
    key=lambda offset: (turns(offset) == 3, -far(offset)),
) + [(0, 0, 0, 0)]
N = len(OFFSETS)
NEAR = [offset for offset in OFFSETS[:-1] if turns(offset) < 3]
COLUMN = [(0, 0, dz, 0) for dz in range(1, 4)]
PER = N // CHUNKS
ROWS = PER * CAP


def place():
    grp, loc = lax.axis_index("grp"), lax.axis_index("loc")
    return grp // 2, grp % 2, loc // 4, loc % 4


def device_at(offset, sign):
    x, c, z, y = place()
    dx, dc, dz, dy = offset
    core = (c + dc) % 2
    way = 1 - 2 * c if sign > 0 else 2 * core - 1
    return (x + way * dx + 4) % 4 * 2 + core, (z + way * dz + 4) % 4 * 4 + (y + way * dy + 4) % 4


def spread(index):
    return index % 4 + index // 4 % 4 * 8 + index // 16 % 2 * 64 + index // 32 * 256


def kernel(
    tokens, ids, gates, table, w_gate, w_up, w_down, out,
    tokens_v, ids_v, gates_v, table_v, gate_v, up_v, down_v, send, recv, ret, back, mix, total,
    load_sem, send_sem, recv_sem, ret_sem, back_sem, own_sem, rest_sem,
):
    barrier = pltpu.get_barrier_semaphore()
    for offset in NEAR:
        pl.semaphore_signal(barrier, 1, device_id=device_at(offset, 1), device_id_type=MESH)
    loads = [
        pltpu.make_async_copy(src, dst, load_sem.at[i])
        for i, (src, dst) in enumerate((
            (ids, ids_v), (table, table_v), (gates, gates_v), (tokens, tokens_v),
            (w_gate.at[0], gate_v), (w_up.at[0], up_v), (w_down.at[0], down_v),
        ))
    ]
    for load in loads:
        load.start()

    x, c, z, y = place()
    for load in loads[:3]:
        load.wait()
    steps = jnp.where(c == 0, table_v[...], ((4 + 4 * 8 + 4 * 256) - (table_v[...] & ~64)) + (table_v[...] & 64))
    expert = (steps + spread(x * 32 + c * 16 + z * 4 + y)) & spread(N - 1)
    asked = spread(ids_v[...])
    first = asked[0:1, :] == expert
    second = asked[1:2, :] == expert
    named = first | second
    rows = tokens.shape[0]
    earlier = lax.broadcasted_iota(jnp.int32, (rows, rows), 0) < lax.broadcasted_iota(jnp.int32, (rows, rows), 1)
    before = jnp.dot(
        named.astype(jnp.bfloat16), earlier.astype(jnp.bfloat16), preferred_element_type=jnp.float32
    )
    slot = lax.broadcasted_iota(jnp.int32, named.shape, 0) % CAP
    chosen = named & (before == slot.astype(jnp.float32))
    pick = chosen.astype(jnp.bfloat16)
    loads[3].wait()
    for k in range(CHUNKS):
        part = jnp.dot(pick[k * ROWS : (k + 1) * ROWS], tokens_v[...], preferred_element_type=jnp.float32)
        send[k * PER : (k + 1) * PER] = part.astype(jnp.bfloat16).reshape(PER, CAP, -1)
        if k == 0:
            pl.semaphore_wait(barrier, len(NEAR))
            for offset in COLUMN:
                pl.semaphore_signal(rest_sem, 1, device_id=device_at(offset, 1), device_id_type=MESH)
        if (k + 1) * PER > len(NEAR) >= k * PER:
            pl.semaphore_wait(rest_sem, len(COLUMN))
        for i in range(k * PER, min((k + 1) * PER, N - 1)):
            pltpu.make_async_remote_copy(
                send.at[i], recv.at[i], send_sem, recv_sem.at[k],
                device_id=device_at(OFFSETS[i], 1), device_id_type=MESH,
            ).start()
    own = pltpu.make_async_copy(send.at[N - 1], recv.at[N - 1], own_sem.at[0])
    own.start()

    fixed = gates_v[...].astype(jnp.float32)
    weights = fixed / jnp.sum(fixed, axis=0, keepdims=True)
    scale = jnp.where(chosen, jnp.where(first, weights[0:1, :], weights[1:2, :]), 0.0).T
    mix[0] = scale.astype(jnp.bfloat16)
    mix[1] = (scale - mix[0].astype(jnp.float32)).astype(jnp.bfloat16)
    for load in loads[4:]:
        load.wait()

    def arrived(buffer, sem, k):
        count = PER - (k == CHUNKS - 1)
        landed = buffer.at[pl.ds(k * PER, count)]
        pltpu.make_async_copy(landed, landed, sem.at[k]).wait()

    for k in range(CHUNKS):
        arrived(recv, recv_sem, k)
        if k == CHUNKS - 1:
            own.wait()
        block = recv[k * PER : (k + 1) * PER].reshape(ROWS, -1)
        gate = jnp.dot(block, gate_v[...], preferred_element_type=jnp.float32)
        upper = jnp.dot(block, up_v[...], preferred_element_type=jnp.float32)
        hidden = (gate / (1.0 + jnp.exp(-gate)) * upper).astype(jnp.bfloat16)
        result = jnp.dot(hidden, down_v[...], preferred_element_type=jnp.float32)
        ret[k * PER : (k + 1) * PER] = result.astype(jnp.bfloat16).reshape(PER, CAP, -1)
        for i in range(k * PER, min((k + 1) * PER, N - 1)):
            pltpu.make_async_remote_copy(
                ret.at[i], back.at[i], ret_sem, back_sem.at[k],
                device_id=device_at(OFFSETS[i], -1), device_id_type=MESH,
            ).start()
    home = pltpu.make_async_copy(ret.at[N - 1], back.at[N - 1], own_sem.at[1])
    home.start()

    for k in range(CHUNKS):
        arrived(back, back_sem, k)
        if k == CHUNKS - 1:
            home.wait()
        block = back[k * PER : (k + 1) * PER].reshape(ROWS, -1)
        columns = slice(k * ROWS, (k + 1) * ROWS)
        part = jnp.dot(mix[0, :, columns], block, preferred_element_type=jnp.float32)
        part = part + jnp.dot(mix[1, :, columns], block, preferred_element_type=jnp.float32)
        if k == CHUNKS - 1:
            out[...] = (total[...] + part).astype(out.dtype)
        else:
            total[...] = part if k == 0 else total[...] + part
    sent = send.at[pl.ds(0, N - 1)]
    pltpu.make_async_copy(sent, sent, send_sem).wait()
    pltpu.make_async_copy(sent, sent, ret_sem).wait()


def body(tokens, expert_ids, gate_fixed, gate_weight, up_weight, down_weight):
    rows, width = tokens.shape
    hidden = gate_weight.shape[2]
    table = np.zeros((N * CAP, rows), np.int32)
    for i, (dx, dc, dz, dy) in enumerate(OFFSETS):
        table[i * CAP : (i + 1) * CAP] = spread(dx * 32 + dc * 16 + dz * 4 + dy)
    vmem = pl.BlockSpec(memory_space=pltpu.VMEM)
    hbm = pl.BlockSpec(memory_space=pl.ANY)
    slots = pltpu.VMEM((N, CAP, width), jnp.bfloat16)
    dma = pltpu.SemaphoreType.DMA
    return pl.pallas_call(
        kernel,
        out_shape=pltpu.VMEM((rows, width), jnp.bfloat16),
        in_specs=[hbm] * 7,
        out_specs=vmem,
        scratch_shapes=[
            pltpu.VMEM((rows, width), jnp.bfloat16),
            pltpu.VMEM((2, rows), jnp.int32),
            pltpu.VMEM((2, rows), jnp.int32),
            pltpu.VMEM((N * CAP, rows), jnp.int32),
            pltpu.VMEM((width, hidden), jnp.bfloat16),
            pltpu.VMEM((width, hidden), jnp.bfloat16),
            pltpu.VMEM((hidden, width), jnp.bfloat16),
            slots, slots, slots, slots,
            pltpu.VMEM((2, rows, N * CAP), jnp.bfloat16),
            pltpu.VMEM((rows, width), jnp.float32),
            dma((7,)), dma, dma((CHUNKS,)), dma, dma((CHUNKS,)), dma((2,)), pltpu.SemaphoreType.REGULAR,
        ],
        compiler_params=pltpu.CompilerParams(
            collective_id=0, has_side_effects=True, vmem_limit_bytes=60 << 20
        ),
    )(tokens, expert_ids.T, gate_fixed.T, jnp.asarray(table), gate_weight, up_weight, down_weight)


def solution(mesh):
    rows = P(("grp", "loc"), None)
    experts = P(("grp", "loc"), None, None)
    return jax.shard_map(
        body, mesh=mesh, in_specs=(rows, rows, rows, experts, experts, experts), out_specs=rows, check_vma=False
    )
```

```python
import functools

import jax
import jax.numpy as jnp
import numpy as np
from jax import lax
from jax.experimental import pallas as pl
from jax.experimental.pallas import tpu as pltpu
from jax.sharding import PartitionSpec as P

MESH = pl.DeviceIdType.MESH
CAP = 4
CHUNKS = 4


def far(offset):
    return sum(min(step, 4 - step) for step in (offset[0], offset[2], offset[3]))


def turns(offset):
    return (offset[0] + offset[1] > 0) + (offset[2] > 0) + (offset[3] > 0)


OFFSETS = sorted(
    ((dx, dc, dz, dy) for dx in range(4) for dc in range(2) for dz in range(4) for dy in range(4) if dx + dc + dz + dy),
    key=lambda offset: -far(offset),
)
NEAR = [offset for offset in OFFSETS if turns(offset) < 3]
EARLY = 32
OFFSETS = NEAR[:EARLY] + [offset for offset in OFFSETS if turns(offset) == 3] + NEAR[EARLY:] + [(0, 0, 0, 0)]
N = len(OFFSETS)
COLUMN = [(0, 0, dz, 0) for dz in range(1, 4)]
PER = N // CHUNKS
ROWS = PER * CAP


def place():
    grp, loc = lax.axis_index("grp"), lax.axis_index("loc")
    return grp // 2, grp % 2, loc // 4, loc % 4


def device_at(offset, sign):
    x, c, z, y = place()
    dx, dc, dz, dy = offset
    core = (c + dc) % 2
    way = 1 - 2 * c if sign > 0 else 2 * core - 1
    return (x + way * dx + 4) % 4 * 2 + core, (z + way * dz + 4) % 4 * 4 + (y + way * dy + 4) % 4


def spread(index):
    return index % 4 + index // 4 % 4 * 8 + index // 16 % 2 * 64 + index // 32 * 256


def kernel(
    tokens, ids, gates, table, w_gate, w_up, w_down, out,
    tokens_v, ids_v, gates_v, table_v, gate_v, up_v, down_v, send, recv, ret, back, mix, total,
    load_sem, send_sem, recv_sem, ret_sem, back_sem, own_sem, rest_sem,
):
    barrier = pltpu.get_barrier_semaphore()
    for offset in NEAR:
        pl.semaphore_signal(barrier, 1, device_id=device_at(offset, 1), device_id_type=MESH)
    loads = [
        pltpu.make_async_copy(src, dst, load_sem.at[i])
        for i, (src, dst) in enumerate((
            (ids, ids_v), (table, table_v), (gates, gates_v), (tokens, tokens_v),
            (w_gate.at[0], gate_v), (w_up.at[0], up_v), (w_down.at[0], down_v),
        ))
    ]
    for load in loads:
        load.start()

    x, c, z, y = place()
    for load in loads[:3]:
        load.wait()
    steps = jnp.where(c == 0, table_v[...], ((4 + 4 * 8 + 4 * 256) - (table_v[...] & ~64)) + (table_v[...] & 64))
    expert = (steps + spread(x * 32 + c * 16 + z * 4 + y)) & spread(N - 1)
    asked = spread(ids_v[...])
    first = asked[0:1, :] == expert
    second = asked[1:2, :] == expert
    named = first | second
    rows = tokens.shape[0]
    earlier = lax.broadcasted_iota(jnp.int32, (rows, rows), 0) < lax.broadcasted_iota(jnp.int32, (rows, rows), 1)
    before = jnp.dot(
        named.astype(jnp.bfloat16), earlier.astype(jnp.bfloat16), preferred_element_type=jnp.float32
    )
    slot = lax.broadcasted_iota(jnp.int32, named.shape, 0) % CAP
    chosen = named & (before == slot.astype(jnp.float32))
    pick = chosen.astype(jnp.bfloat16)
    loads[3].wait()
    for k in range(CHUNKS):
        part = jnp.dot(pick[k * ROWS : (k + 1) * ROWS], tokens_v[...], preferred_element_type=jnp.float32)
        send[k * PER : (k + 1) * PER] = part.astype(jnp.bfloat16).reshape(PER, CAP, -1)
        if k == 0:
            pl.semaphore_wait(barrier, len(NEAR))
            for offset in COLUMN:
                pl.semaphore_signal(rest_sem, 1, device_id=device_at(offset, 1), device_id_type=MESH)
        if (k + 1) * PER > EARLY >= k * PER:
            pl.semaphore_wait(rest_sem, len(COLUMN))
        for i in range(k * PER, min((k + 1) * PER, N - 1)):
            pltpu.make_async_remote_copy(
                send.at[i], recv.at[i], send_sem, recv_sem.at[k],
                device_id=device_at(OFFSETS[i], 1), device_id_type=MESH,
            ).start()
    own = pltpu.make_async_copy(send.at[N - 1], recv.at[N - 1], own_sem.at[0])
    own.start()

    fixed = gates_v[...].astype(jnp.float32)
    weights = fixed / jnp.sum(fixed, axis=0, keepdims=True)
    scale = jnp.where(chosen, jnp.where(first, weights[0:1, :], weights[1:2, :]), 0.0).T
    mix[0] = scale.astype(jnp.bfloat16)
    mix[1] = (scale - mix[0].astype(jnp.float32)).astype(jnp.bfloat16)
    for load in loads[4:]:
        load.wait()

    def arrived(buffer, sem, k):
        count = PER - (k == CHUNKS - 1)
        landed = buffer.at[pl.ds(k * PER, count)]
        pltpu.make_async_copy(landed, landed, sem.at[k]).wait()

    for k in range(CHUNKS):
        arrived(recv, recv_sem, k)
        if k == CHUNKS - 1:
            own.wait()
        block = recv[k * PER : (k + 1) * PER].reshape(ROWS, -1)
        gate = jnp.dot(block, gate_v[...], preferred_element_type=jnp.float32)
        upper = jnp.dot(block, up_v[...], preferred_element_type=jnp.float32)
        hidden = (gate / (1.0 + jnp.exp(-gate)) * upper).astype(jnp.bfloat16)
        result = jnp.dot(hidden, down_v[...], preferred_element_type=jnp.float32)
        ret[k * PER : (k + 1) * PER] = result.astype(jnp.bfloat16).reshape(PER, CAP, -1)
        for i in range(k * PER, min((k + 1) * PER, N - 1)):
            pltpu.make_async_remote_copy(
                ret.at[i], back.at[i], ret_sem, back_sem.at[k],
                device_id=device_at(OFFSETS[i], -1), device_id_type=MESH,
            ).start()
    home = pltpu.make_async_copy(ret.at[N - 1], back.at[N - 1], own_sem.at[1])
    home.start()

    for k in range(CHUNKS):
        arrived(back, back_sem, k)
        if k == CHUNKS - 1:
            home.wait()
        block = back[k * PER : (k + 1) * PER].reshape(ROWS, -1)
        columns = slice(k * ROWS, (k + 1) * ROWS)
        part = jnp.dot(mix[0, :, columns], block, preferred_element_type=jnp.float32)
        part = part + jnp.dot(mix[1, :, columns], block, preferred_element_type=jnp.float32)
        if k == CHUNKS - 1:
            out[...] = (total[...] + part).astype(out.dtype)
        else:
            total[...] = part if k == 0 else total[...] + part
    sent = send.at[pl.ds(0, N - 1)]
    pltpu.make_async_copy(sent, sent, send_sem).wait()
    pltpu.make_async_copy(sent, sent, ret_sem).wait()


def body(tokens, expert_ids, gate_fixed, gate_weight, up_weight, down_weight):
    rows, width = tokens.shape
    hidden = gate_weight.shape[2]
    table = np.zeros((N * CAP, rows), np.int32)
    for i, (dx, dc, dz, dy) in enumerate(OFFSETS):
        table[i * CAP : (i + 1) * CAP] = spread(dx * 32 + dc * 16 + dz * 4 + dy)
    vmem = pl.BlockSpec(memory_space=pltpu.VMEM)
    hbm = pl.BlockSpec(memory_space=pl.ANY)
    slots = pltpu.VMEM((N, CAP, width), jnp.bfloat16)
    dma = pltpu.SemaphoreType.DMA
    return pl.pallas_call(
        kernel,
        out_shape=pltpu.VMEM((rows, width), jnp.bfloat16),
        in_specs=[hbm] * 7,
        out_specs=vmem,
        scratch_shapes=[
            pltpu.VMEM((rows, width), jnp.bfloat16),
            pltpu.VMEM((2, rows), jnp.int32),
            pltpu.VMEM((2, rows), jnp.int32),
            pltpu.VMEM((N * CAP, rows), jnp.int32),
            pltpu.VMEM((width, hidden), jnp.bfloat16),
            pltpu.VMEM((width, hidden), jnp.bfloat16),
            pltpu.VMEM((hidden, width), jnp.bfloat16),
            slots, slots, slots, slots,
            pltpu.VMEM((2, rows, N * CAP), jnp.bfloat16),
            pltpu.VMEM((rows, width), jnp.float32),
            dma((7,)), dma, dma((CHUNKS,)), dma, dma((CHUNKS,)), dma((2,)), pltpu.SemaphoreType.REGULAR,
        ],
        compiler_params=pltpu.CompilerParams(
            collective_id=0, has_side_effects=True, vmem_limit_bytes=60 << 20
        ),
    )(tokens, expert_ids.T, gate_fixed.T, jnp.asarray(table), gate_weight, up_weight, down_weight)


def solution(mesh):
    rows = P(("grp", "loc"), None)
    experts = P(("grp", "loc"), None, None)
    return jax.shard_map(
        body, mesh=mesh, in_specs=(rows, rows, rows, experts, experts, experts), out_specs=rows, check_vma=False
    )
```

```python
import functools

import jax
import jax.numpy as jnp
import numpy as np
from jax import lax
from jax.experimental import pallas as pl
from jax.experimental.pallas import tpu as pltpu
from jax.sharding import PartitionSpec as P

MESH = pl.DeviceIdType.MESH
CAP = 4
CHUNKS = 4


def far(offset):
    return sum(min(step, 4 - step) for step in (offset[0], offset[2], offset[3]))


def turns(offset):
    return (offset[0] + offset[1] > 0) + (offset[2] > 0) + (offset[3] > 0)


OFFSETS = sorted(
    ((dx, dc, dz, dy) for dx in range(4) for dc in range(2) for dz in range(4) for dy in range(4) if dx + dc + dz + dy),
    key=lambda offset: -far(offset),
)
NEAR = [offset for offset in OFFSETS if turns(offset) < 3]
EARLY = 32
OFFSETS = NEAR[:EARLY] + [offset for offset in OFFSETS if turns(offset) == 3] + NEAR[EARLY:] + [(0, 0, 0, 0)]
N = len(OFFSETS)
GREET = [offset for i, offset in enumerate(NEAR) if i < EARLY or offset[2] == 0 or offset[:2] + offset[3:] == (0, 0, 0)]
COLUMN = [(0, 0, dz, 0) for dz in range(1, 4)]
PER = N // CHUNKS
ROWS = PER * CAP


def place():
    grp, loc = lax.axis_index("grp"), lax.axis_index("loc")
    return grp // 2, grp % 2, loc // 4, loc % 4


def device_at(offset, sign):
    x, c, z, y = place()
    dx, dc, dz, dy = offset
    core = (c + dc) % 2
    way = 1 - 2 * c if sign > 0 else 2 * core - 1
    return (x + way * dx + 4) % 4 * 2 + core, (z + way * dz + 4) % 4 * 4 + (y + way * dy + 4) % 4


def spread(index):
    return index % 4 + index // 4 % 4 * 8 + index // 16 % 2 * 64 + index // 32 * 256


def kernel(
    tokens, ids, gates, table, w_gate, w_up, w_down, out,
    tokens_v, ids_v, gates_v, table_v, gate_v, up_v, down_v, send, recv, ret, back, mix, total,
    load_sem, send_sem, recv_sem, ret_sem, back_sem, own_sem, rest_sem,
):
    barrier = pltpu.get_barrier_semaphore()
    for offset in GREET:
        pl.semaphore_signal(barrier, 1, device_id=device_at(offset, -1), device_id_type=MESH)
    loads = [
        pltpu.make_async_copy(src, dst, load_sem.at[i])
        for i, (src, dst) in enumerate((
            (ids, ids_v), (table, table_v), (gates, gates_v), (tokens, tokens_v),
            (w_gate.at[0], gate_v), (w_up.at[0], up_v), (w_down.at[0], down_v),
        ))
    ]
    for load in loads:
        load.start()

    x, c, z, y = place()
    for load in loads[:3]:
        load.wait()
    steps = jnp.where(c == 0, table_v[...], ((4 + 4 * 8 + 4 * 256) - (table_v[...] & ~64)) + (table_v[...] & 64))
    expert = (steps + spread(x * 32 + c * 16 + z * 4 + y)) & spread(N - 1)
    asked = spread(ids_v[...])
    first = asked[0:1, :] == expert
    second = asked[1:2, :] == expert
    named = first | second
    rows = tokens.shape[0]
    earlier = lax.broadcasted_iota(jnp.int32, (rows, rows), 0) < lax.broadcasted_iota(jnp.int32, (rows, rows), 1)
    before = jnp.dot(
        named.astype(jnp.bfloat16), earlier.astype(jnp.bfloat16), preferred_element_type=jnp.float32
    )
    slot = lax.broadcasted_iota(jnp.int32, named.shape, 0) % CAP
    chosen = named & (before == slot.astype(jnp.float32))
    pick = chosen.astype(jnp.bfloat16)
    loads[3].wait()
    for k in range(CHUNKS):
        part = jnp.dot(pick[k * ROWS : (k + 1) * ROWS], tokens_v[...], preferred_element_type=jnp.float32)
        send[k * PER : (k + 1) * PER] = part.astype(jnp.bfloat16).reshape(PER, CAP, -1)
        if k == 0:
            pl.semaphore_wait(barrier, len(GREET))
            for offset in COLUMN:
                pl.semaphore_signal(rest_sem, 1, device_id=device_at(offset, 1), device_id_type=MESH)
        if (k + 1) * PER > EARLY >= k * PER:
            pl.semaphore_wait(rest_sem, len(COLUMN))
        for i in range(k * PER, min((k + 1) * PER, N - 1)):
            pltpu.make_async_remote_copy(
                send.at[i], recv.at[i], send_sem, recv_sem.at[k],
                device_id=device_at(OFFSETS[i], 1), device_id_type=MESH,
            ).start()
    own = pltpu.make_async_copy(send.at[N - 1], recv.at[N - 1], own_sem.at[0])
    own.start()

    fixed = gates_v[...].astype(jnp.float32)
    weights = fixed / jnp.sum(fixed, axis=0, keepdims=True)
    scale = jnp.where(chosen, jnp.where(first, weights[0:1, :], weights[1:2, :]), 0.0).T
    mix[0] = scale.astype(jnp.bfloat16)
    mix[1] = (scale - mix[0].astype(jnp.float32)).astype(jnp.bfloat16)
    for load in loads[4:]:
        load.wait()

    def arrived(buffer, sem, k):
        count = PER - (k == CHUNKS - 1)
        landed = buffer.at[pl.ds(k * PER, count)]
        pltpu.make_async_copy(landed, landed, sem.at[k]).wait()

    for k in range(CHUNKS):
        arrived(recv, recv_sem, k)
        if k == CHUNKS - 1:
            own.wait()
        block = recv[k * PER : (k + 1) * PER].reshape(ROWS, -1)
        gate = jnp.dot(block, gate_v[...], preferred_element_type=jnp.float32)
        upper = jnp.dot(block, up_v[...], preferred_element_type=jnp.float32)
        hidden = (gate / (1.0 + jnp.exp(-gate)) * upper).astype(jnp.bfloat16)
        result = jnp.dot(hidden, down_v[...], preferred_element_type=jnp.float32)
        ret[k * PER : (k + 1) * PER] = result.astype(jnp.bfloat16).reshape(PER, CAP, -1)
        for i in range(k * PER, min((k + 1) * PER, N - 1)):
            pltpu.make_async_remote_copy(
                ret.at[i], back.at[i], ret_sem, back_sem.at[k],
                device_id=device_at(OFFSETS[i], -1), device_id_type=MESH,
            ).start()
    home = pltpu.make_async_copy(ret.at[N - 1], back.at[N - 1], own_sem.at[1])
    home.start()

    for k in range(CHUNKS):
        arrived(back, back_sem, k)
        if k == CHUNKS - 1:
            home.wait()
        block = back[k * PER : (k + 1) * PER].reshape(ROWS, -1)
        columns = slice(k * ROWS, (k + 1) * ROWS)
        part = jnp.dot(mix[0, :, columns], block, preferred_element_type=jnp.float32)
        part = part + jnp.dot(mix[1, :, columns], block, preferred_element_type=jnp.float32)
        if k == CHUNKS - 1:
            out[...] = (total[...] + part).astype(out.dtype)
        else:
            total[...] = part if k == 0 else total[...] + part
    sent = send.at[pl.ds(0, N - 1)]
    pltpu.make_async_copy(sent, sent, send_sem).wait()
    pltpu.make_async_copy(sent, sent, ret_sem).wait()


def body(tokens, expert_ids, gate_fixed, gate_weight, up_weight, down_weight):
    rows, width = tokens.shape
    hidden = gate_weight.shape[2]
    table = np.zeros((N * CAP, rows), np.int32)
    for i, (dx, dc, dz, dy) in enumerate(OFFSETS):
        table[i * CAP : (i + 1) * CAP] = spread(dx * 32 + dc * 16 + dz * 4 + dy)
    vmem = pl.BlockSpec(memory_space=pltpu.VMEM)
    hbm = pl.BlockSpec(memory_space=pl.ANY)
    slots = pltpu.VMEM((N, CAP, width), jnp.bfloat16)
    dma = pltpu.SemaphoreType.DMA
    return pl.pallas_call(
        kernel,
        out_shape=pltpu.VMEM((rows, width), jnp.bfloat16),
        in_specs=[hbm] * 7,
        out_specs=vmem,
        scratch_shapes=[
            pltpu.VMEM((rows, width), jnp.bfloat16),
            pltpu.VMEM((2, rows), jnp.int32),
            pltpu.VMEM((2, rows), jnp.int32),
            pltpu.VMEM((N * CAP, rows), jnp.int32),
            pltpu.VMEM((width, hidden), jnp.bfloat16),
            pltpu.VMEM((width, hidden), jnp.bfloat16),
            pltpu.VMEM((hidden, width), jnp.bfloat16),
            slots, slots, slots, slots,
            pltpu.VMEM((2, rows, N * CAP), jnp.bfloat16),
            pltpu.VMEM((rows, width), jnp.float32),
            dma((7,)), dma, dma((CHUNKS,)), dma, dma((CHUNKS,)), dma((2,)), pltpu.SemaphoreType.REGULAR,
        ],
        compiler_params=pltpu.CompilerParams(
            collective_id=0, has_side_effects=True, vmem_limit_bytes=60 << 20
        ),
    )(tokens, expert_ids.T, gate_fixed.T, jnp.asarray(table), gate_weight, up_weight, down_weight)


def solution(mesh):
    rows = P(("grp", "loc"), None)
    experts = P(("grp", "loc"), None, None)
    return jax.shard_map(
        body, mesh=mesh, in_specs=(rows, rows, rows, experts, experts, experts), out_specs=rows, check_vma=False
    )
```
